256 devices in a mesh: slab: 64 (over x, z, y_hi), head: 4 (over y_lo, core).
Axes of the slice: x: 4, y: 4 (y_hi: 2, y_lo: 2; y = y_hi * 2 + y_lo), z: 8, core: 2. Of those that a mesh axis runs over, the one named last changes fastest.
Arguments:
- queries: bfloat16 [24576, 3072], P(('slab', 'head')), may hold values from -200 to 200
- keys: bfloat16 [24576, 3072], P(('slab', 'head')), may hold values from -6 to 6
- values: bfloat16 [24576, 3072], P(('slab', 'head')), may hold values from -48 to 48
- windows: int32 [24, 3], replicated, may hold values from 0 to 1
Outputs:
- attended: bfloat16 [24576, 3072], P(('slab', 'head'))
The draws below stay inside these ranges and needn't reach their ends.
All inputs are finite; a program needn't handle non-finite values.
Results may differ from the reference program's by a relative error of at most 0.0049.
Values may be sent and summed in bfloat16 or wider, within the bound.
A program may use at most 128 MiB of HBM per device.

```python
import jax
import jax.numpy as jnp
from jax import lax

HEADS = 24
HD = 128
TILE = 384
TTILES = 2
HTILES = 4
WTILES = 8
TOKENS = 24576


def shared_base(key):
    base = jax.random.normal(jax.random.fold_in(key, 101), (TOKENS, HEADS * HD), jnp.float32)
    return jnp.clip(base, -6.0, 6.0)


def draw_keys(key, part):
    base = shared_base(key)
    return base.astype(jnp.bfloat16)


def draw_queries(key, part):
    key = jax.random.fold_in(key, 5)
    fresh = jnp.clip(jax.random.normal(key, (TOKENS, HEADS * HD), jnp.float32), -6.0, 6.0)
    return fresh.astype(jnp.bfloat16)


def draw_windows(key, part):
    key = jax.random.fold_in(key, 7)
    first, second = jax.random.split(key)
    reach = jax.random.randint(first, (HEADS, 3), 0, 2, dtype=jnp.int32)
    chosen = jax.random.randint(second, (), 0, HEADS, dtype=jnp.int32)
    rows = jnp.arange(HEADS, dtype=jnp.int32)[:, None]
    return jnp.where(rows == chosen, jnp.int32(1), reach).astype(jnp.int32)


def block_levels(rng, shape, cuts, smallest, largest):
    def one(position, parts):
        draws = jax.random.uniform(jax.random.fold_in(jax.random.fold_in(rng, 6), position), (parts,), jnp.float32, smallest / len(cuts), largest / len(cuts))
        return jnp.repeat(jnp.exp(draws), shape[position] // parts).reshape((-1,) + (1,) * (len(shape) - position - 1))

    factor_of = one(*cuts[0])
    for cut in cuts[1:]:
        factor_of = factor_of * one(*cut)
    return factor_of


def gaussian(own_key, shape, width, most, pieces=(), kind=jnp.bfloat16):
    drawn = jax.random.normal(own_key, shape, jnp.float32) * width
    if len(pieces) > 0:
        drawn = block_levels(own_key, shape, pieces, -0.22, 0.18) * drawn
    return jnp.clip(drawn, min=-most, max=most).astype(kind)


def setup_inputs(seed: int = 0) -> dict:
    seeds = jax.random.split(jax.random.key(seed), 5)
    return {
        "queries": draw_queries(jax.random.fold_in(seeds[4], 71), 0),
        "keys": draw_keys(jax.random.fold_in(seeds[4], 71), 0),
        "values": gaussian(seeds[2], (TOKENS, HEADS * HD), 8.0, 48.0, ((0, 256),)),
        "windows": draw_windows(jax.random.fold_in(seeds[4], 71), 0),
    }


def reference(queries, keys, values, windows):
    scale = HD ** -0.5
    shape_six = (TTILES, HTILES, WTILES, TILE, HEADS, HD)
    q_grid = queries.reshape(shape_six)
    padding = ((0, 0), (1, 1), (1, 1), (0, 0), (0, 0), (0, 0))
    k_grid = jnp.pad(keys.reshape(shape_six), padding)
    v_grid = jnp.pad(values.reshape(shape_six), padding)
    offsets = jnp.arange(3, dtype=jnp.int32) - 1
    distance = jnp.abs(offsets)
    t_all = jnp.arange(TTILES, dtype=jnp.int32)
    reach_t = windows[:, 0]
    reach_h = windows[:, 1]
    reach_w = windows[:, 2]
    anchor = jnp.zeros((), jnp.int32)

    def one_tile(index):
        t_pos = (index // (HTILES * WTILES)).astype(jnp.int32)
        h_pos = ((index // WTILES) % HTILES).astype(jnp.int32)
        w_pos = (index % WTILES).astype(jnp.int32)
        q_tile = lax.dynamic_slice(q_grid, (t_pos, h_pos, w_pos, anchor, anchor, anchor), (1, 1, 1, TILE, HEADS, HD))[0, 0, 0].astype(jnp.float32)
        near_shape = (TTILES, 3, 3, TILE, HEADS, HD)
        k_near = lax.dynamic_slice(k_grid, (anchor, h_pos, w_pos, anchor, anchor, anchor), near_shape).reshape(TTILES * 9 * TILE, HEADS, HD).astype(jnp.float32)
        v_near = lax.dynamic_slice(v_grid, (anchor, h_pos, w_pos, anchor, anchor, anchor), near_shape).reshape(TTILES * 9 * TILE, HEADS, HD).astype(jnp.float32)
        t_ok = jnp.abs(t_all - t_pos)[None, :] <= reach_t[:, None]
        h_in = (h_pos + offsets >= 0) & (h_pos + offsets < HTILES)
        w_in = (w_pos + offsets >= 0) & (w_pos + offsets < WTILES)
        h_ok = h_in[None, :] & (distance[None, :] <= reach_h[:, None])
        w_ok = w_in[None, :] & (distance[None, :] <= reach_w[:, None])
        allowed = t_ok[:, :, None, None] & h_ok[:, None, :, None] & w_ok[:, None, None, :]
        keep = jnp.repeat(allowed.reshape(HEADS, TTILES * 9), TILE, axis=1, total_repeat_length=TTILES * 9 * TILE)
        scores = jnp.einsum("qhd,khd->hqk", q_tile, k_near) * scale
        scores = jnp.where(keep[:, None, :], scores, -1.0e30)
        top = jnp.max(scores, axis=2, keepdims=True)
        expo = jnp.exp(scores - top)
        weights = (expo / jnp.sum(expo, axis=2, keepdims=True)).astype(jnp.bfloat16)
        weights = lax.optimization_barrier(weights).astype(jnp.float32)
        output = jnp.einsum("hqk,khd->qhd", weights, v_near)
        return output.astype(jnp.bfloat16).reshape(TILE, HEADS * HD)

    tiles = lax.map(one_tile, jnp.arange(TTILES * HTILES * WTILES, dtype=jnp.int32))
    return tiles.reshape(TOKENS, HEADS * HD)
```

```python
import functools

import jax
import jax.numpy as jnp
from jax import lax
from jax.experimental import pallas as pl
from jax.experimental.pallas import tpu as pltpu
from jax.sharding import PartitionSpec as P

MESH = pl.DeviceIdType.MESH
ANY = pl.BlockSpec(memory_space=pl.ANY)
SMEM = pl.BlockSpec(memory_space=pltpu.SMEM)
VMEM = pl.BlockSpec(memory_space=pltpu.VMEM)
HEADS, HD, TILE, PART = 24, 128, 384, 96
SLOTS, CHIPS = 3, 8
LOG2E = 1.4426950408889634


def coords():
    slab, head = lax.axis_index("slab"), lax.axis_index("head")
    x, z, y_hi = slab // 16, (slab // 2) % 8, slab % 2
    return x, y_hi * 2 + head // 2, z, head % 2


def device(x, y, z, c):
    return ((x * 8 + z) * 2 + y // 2, (y % 2) * 2 + c)


def remote(src, dst, send, recv, to):
    return pltpu.make_async_remote_copy(
        src_ref=src, dst_ref=dst, send_sem=send, recv_sem=recv, device_id=to, device_id_type=MESH
    )


def greet(devices):
    barrier = pltpu.get_barrier_semaphore()
    for to in devices:
        pl.semaphore_signal(barrier, 1, device_id=to, device_id_type=MESH)
    pl.semaphore_wait(barrier, len(devices))


def group(x, y, z, c):
    return [
        device((x + 2 * i) % 4, (y + m) % 4, z, (c + n) % 2)
        for i in range(2)
        for m in range(4)
        for n in range(2)
        if (i, m, n) != (0, 0, 0)
    ]


def pack_kernel(rank, q_in, k_in, v_in, q_out, kv_out):
    for e in range(HEADS):
        r = rank[e]
        cols = pl.ds(e * HD, HD)
        q_out[r] = q_in[:, cols]
        kv_out[r, 0] = k_in[:, cols]
        kv_out[r, 1] = v_in[:, cols]


def unpack_kernel(rank, o_in, out):
    for e in range(HEADS):
        out[:, e * HD : (e + 1) * HD] = o_in[rank[e]]


def gather_kernel(
    far, qh, kvh, q, kv, relay, a_send, q_send, kv_recv, q_recv, hop_send, hop_recv, own_send, own_recv,
    mid_send, mid_recv, x_send, x_recv, xs_send, xs_recv,
):
    x, y, z, c = coords()
    z_hi, x_lo, t = z // 4, x % 2, x // 2
    up, down = (z + 1) % 8, (z + 7) % 8
    twin = device(x, y, z, 1 - c)
    side = device(x + 1 - 2 * x_lo, y, z, c)
    ahead = device(x, y, jnp.where(c == 0, up, down), c)
    first = device(x, y, jnp.where(c == 0, down, up), 1 - c)
    greet(
        group(x, y, z, c)
        + [device(x, y, up, c), device(x, y, up, 1 - c), device(x, y, down, c), device(x, y, down, 1 - c), side]
    )

    y_hi = y // 2
    part = (y % 2) * 2 + c
    me = t * 4 + y
    rows = pl.ds(part * PART, PART)
    copies = []

    def send(src, dst, sem, recv, chip):
        alone = (chip == me) & (c == y_hi)
        to = device((chip // 4) * 2 + x_lo, chip % 4, z, y_hi)

        @pl.when(alone)
        def _():
            pltpu.make_async_copy(src, dst, recv).start()

        @pl.when(jnp.logical_not(alone))
        def _():
            remote(src, dst, sem, recv, to).start()

        copies.append((alone, remote(src, dst, sem, recv, to)))

    for k in range(SLOTS):
        for i in range(CHIPS):
            chip = (me + i) % CHIPS
            send(kvh.at[k, chip], kv.at[k, 1, 1, :, t, rows], a_send.at[k, i], kv_recv.at[k], chip)
    for i in range(CHIPS):
        chip = (me + i) % CHIPS
        send(qh.at[:, chip], q.at[:, t, rows], q_send.at[i], q_recv, chip)

    outer = c * 2
    inner = 2 - outer
    near = 2 - 2 * z_hi
    z_next = jnp.where(c == 0, up, down)
    near_next = 2 - 2 * (z_next // 4)
    started = []

    def go(copy):
        copy.start()
        started.append(copy)

    def landing(k, hop, part, near_of):
        if hop == 1:
            return kv.at[k, 1, outer, part]
        if hop < 4:
            return relay.at[k, hop - 2, part]
        return kv.at[k, near_of, inner if hop == 4 else outer, part]

    def hop_wait(k, hop, part):
        place = landing(k, hop, part, near)
        pltpu.make_async_copy(place, place, hop_recv.at[k, hop - 1, part]).wait()

    def wait_for(place, sem):
        pltpu.make_async_copy(place, place, sem).wait()

    def begin(k):
        own = kv.at[k, 1, 1]
        wait_for(own, kv_recv.at[k])
        for part in range(2):
            go(remote(kv.at[k, 1, 1, part], kv.at[k, 1, inner, part], hop_send.at[k, 0, part], hop_recv.at[k, 0, part], first))
        go(remote(own, kv.at[k, 1, outer], own_send.at[k], own_recv.at[k], twin))

    def forward(k, hop):
        for part in range(2):
            hop_wait(k, hop - 1, part)
            go(
                remote(
                    landing(k, hop - 1, part, near),
                    landing(k, hop, part, near_next),
                    hop_send.at[k, hop - 1, part],
                    hop_recv.at[k, hop - 1, part],
                    ahead,
                )
            )

    sender = x_lo == z_hi
    side_copies = []

    def aside(k, n, place):
        copy = remote(kv.at[k, near, place], kv.at[k, 2 - near, place], x_send.at[k, n], x_recv.at[k, n], side)
        side_copies.append(copy)
        pl.when(sender)(copy.start)

    def middle(k):
        go(remote(kv.at[k, near, inner], kv.at[k, near, 1], mid_send.at[k], mid_recv.at[k], twin))
        aside(k, 0, inner)

    def finish(k):
        for part in range(2):
            hop_wait(k, 5, part)
        aside(k, 1, outer)

    def side_share(k):
        share = remote(kv.at[k, 2 - near, inner], kv.at[k, 2 - near, 1], xs_send.at[k], xs_recv.at[k], twin)
        side_copies.append(share)

        @pl.when(jnp.logical_not(sender))
        def _():
            wait_for(kv.at[k, 2 - near, inner], x_recv.at[k, 0])
            share.start()

    begin(0)
    begin(1)
    for k in range(far):
        forward(k, 2)
        if k > 0:
            finish(k - 1)
        forward(k, 3)
        if k == 0:
            begin(2)
        forward(k, 4)
        if k > 0:
            side_share(k - 1)
        forward(k, 5)
        middle(k)
    if far == 0:
        begin(2)
    else:
        finish(far - 1)
        side_share(far - 1)

    for k in range(SLOTS):
        if k >= far:
            for part in range(2):
                hop_wait(k, 1, part)
        else:
            wait_for(kv.at[k, near, 1], mid_recv.at[k])
        wait_for(kv.at[k, 1, inner], own_recv.at[k])
    wait_for(q, q_recv)
    for alone, copy in copies:
        pl.when(jnp.logical_not(alone))(copy.wait_send)
    for copy in started:
        copy.wait_send()
    for k in range(far):

        @pl.when(sender)
        def _():
            for n in range(2):
                place = kv.at[k, near, inner if n == 0 else outer]
                remote(place, place, x_send.at[k, n], x_recv.at[k, n], side).wait_send()

        @pl.when(jnp.logical_not(sender))
        def _():
            place = kv.at[k, 2 - near, inner]
            remote(place, place, xs_send.at[k], xs_recv.at[k], twin).wait_send()
            wait_for(kv.at[k, 2 - near, outer], x_recv.at[k, 1])
            wait_for(kv.at[k, 2 - near, 1], xs_recv.at[k])


def gather(far, qh, kvh):
    dma = pltpu.SemaphoreType.DMA
    return pl.pallas_call(
        functools.partial(gather_kernel, far),
        out_shape=(
            jax.ShapeDtypeStruct((SLOTS, 2, TILE, HD), jnp.bfloat16),
            jax.ShapeDtypeStruct((SLOTS, 3, 3, 2, 2, TILE, HD), jnp.bfloat16),
        ),
        in_specs=[ANY, ANY],
        out_specs=(ANY, ANY),
        scratch_shapes=[
            pltpu.VMEM((SLOTS, 2, 2, 2, TILE, HD), jnp.bfloat16),
            dma((SLOTS, CHIPS)),
            dma((CHIPS,)),
            dma((SLOTS,)),
            dma,
            dma((SLOTS, 5, 2)),
            dma((SLOTS, 5, 2)),
            dma((SLOTS,)),
            dma((SLOTS,)),
            dma((SLOTS,)),
            dma((SLOTS,)),
            dma((SLOTS, 2)),
            dma((SLOTS, 2)),
            dma((SLOTS,)),
            dma((SLOTS,)),
        ],
        compiler_params=pltpu.CompilerParams(collective_id=far, has_side_effects=True, vmem_limit_bytes=32 << 20),
        name=f"gather{far}",
    )(qh, kvh)


def attend_kernel(reach, q_hbm, kv_hbm, out, q, kv, q_sem, kv_sem, top, total, acc):
    x, y, z, c = coords()
    h, w = (x % 2) * 2 + z // 4, (z % 4) * 2 + c
    chip = (x // 2) * 4 + y
    load_q = pltpu.make_async_copy(q_hbm, q, q_sem)
    load_q.start()
    order = [(1, 1), (1, 0), (1, 2), (0, 1), (0, 0), (0, 2), (2, 1), (2, 0), (2, 2)]

    def allowed(k, dh, dw):
        row = k * CHIPS + chip
        ok_h = (dh == 1) | ((reach[row, 1] > 0) & (h + dh - 1 >= 0) & (h + dh - 1 < 4))
        ok_w = (dw == 1) | ((reach[row, 2] > 0) & (w + dw - 1 >= 0) & (w + dw - 1 < 8))
        return ok_h & ok_w

    def load(k, dh, dw):
        return pltpu.make_async_copy(kv_hbm.at[k, dh, dw], kv.at[k, dh, dw], kv_sem.at[k, dh, dw])

    for k in range(SLOTS):
        for dh, dw in order:
            pl.when(allowed(k, dh, dw))(load(k, dh, dw).start)
    load_q.wait()
    scale = HD ** (-0.5) * LOG2E
    QB = 128

    def update(k, t, keys, vals):
        for b in range(TILE // QB):
            rows = pl.ds(t * TILE + b * QB, QB)
            query = q[k, t, b * QB : (b + 1) * QB]
            s = lax.dot_general(query, keys, (((1,), (1,)), ((), ())), preferred_element_type=jnp.float32)
            old = top[rows]
            new = jnp.maximum(old, jnp.max(s, axis=1, keepdims=True))
            p = jnp.exp2(s * scale - new[:, :1] * scale)
            fix = jnp.exp2((old - new) * scale)
            total[rows] = total[rows] * fix + jnp.sum(p, axis=1, keepdims=True)
            acc[rows] = acc[rows] * fix + jnp.dot(p.astype(jnp.bfloat16), vals, preferred_element_type=jnp.float32)
            top[rows] = new

    def one_head(k, carry):
        top[...] = jnp.full_like(top, -1e30)
        total[...] = jnp.zeros_like(total)
        acc[...] = jnp.zeros_like(acc)
        both = reach[k * CHIPS + chip, 0] > 0

        def one_tile(n, carry):
            dh, dw = (n // 3 + 1) % 3, (n % 3 + 1) % 3

            @pl.when(allowed(k, dh, dw))
            def _():
                load(k, dh, dw).wait()

                @pl.when(both)
                def _():
                    keys = kv[k, dh, dw, 0].reshape(2 * TILE, HD)
                    vals = kv[k, dh, dw, 1].reshape(2 * TILE, HD)
                    for t in range(2):
                        update(k, t, keys, vals)

                @pl.when(jnp.logical_not(both))
                def _():
                    for t in range(2):
                        update(k, t, kv[k, dh, dw, 0, t], kv[k, dh, dw, 1, t])

            return carry

        lax.fori_loop(0, 9, one_tile, 0)
        result = acc[...] / total[...]
        out[k] = result.astype(jnp.bfloat16).reshape(2, TILE, HD)
        return carry

    lax.fori_loop(0, SLOTS, one_head, 0)


def attend(reach, q, kv):
    dma = pltpu.SemaphoreType.DMA
    return pl.pallas_call(
        attend_kernel,
        out_shape=jax.ShapeDtypeStruct((SLOTS, 2, TILE, HD), jnp.bfloat16),
        in_specs=[SMEM, ANY, ANY],
        out_specs=VMEM,
        scratch_shapes=[
            pltpu.VMEM((SLOTS, 2, TILE, HD), jnp.bfloat16),
            pltpu.VMEM((SLOTS, 3, 3, 2, 2, TILE, HD), jnp.bfloat16),
            dma,
            dma((SLOTS, 3, 3)),
            pltpu.VMEM((2 * TILE, HD), jnp.float32),
            pltpu.VMEM((2 * TILE, HD), jnp.float32),
            pltpu.VMEM((2 * TILE, HD), jnp.float32),
        ],
        compiler_params=pltpu.CompilerParams(vmem_limit_bytes=40 << 20),
        name="attend",
    )(reach, q, kv)


def return_kernel(o, back, send_sem, recv_sem):
    x, y, z, c = coords()
    x_lo = x % 2
    chip = (x // 2) * 4 + y
    greet(group(x, y, z, c))
    mine = (x // 2) * 4 + (y % 2) * 2 + c
    home = y // 2 == c
    copies = []
    for i in range(8):
        n = (mine + i) % 8
        t, part = n // 4, n % 4
        to = device(t * 2 + x_lo, c * 2 + part // 2, z, part % 2)
        src = o.at[:, t, pl.ds(part * PART, PART)]
        dst = back.at[:, chip]
        copy = remote(src, dst, send_sem.at[i], recv_sem, to)
        if i == 0:
            pl.when(home)(pltpu.make_async_copy(src, dst, recv_sem).start)
            pl.when(jnp.logical_not(home))(copy.start)
        else:
            copy.start()
        copies.append(copy)
    pltpu.make_async_copy(back, back, recv_sem).wait()
    for i, copy in enumerate(copies):
        if i == 0:
            pl.when(jnp.logical_not(home))(copy.wait_send)
        else:
            copy.wait_send()


def give_back(o):
    dma = pltpu.SemaphoreType.DMA
    return pl.pallas_call(
        return_kernel,
        out_shape=jax.ShapeDtypeStruct((SLOTS, CHIPS, PART, HD), jnp.bfloat16),
        in_specs=[ANY],
        out_specs=ANY,
        scratch_shapes=[dma((8,)), dma],
        compiler_params=pltpu.CompilerParams(collective_id=8, has_side_effects=True),
        name="give_back",
    )(o)


def shards(queries, keys, values, windows):
    weight = windows[:, 1] * 4 + windows[:, 2] * 2 + windows[:, 0]
    index = jnp.arange(HEADS, dtype=jnp.int32)
    ahead = (weight[None, :] > weight[:, None]) | ((weight[None, :] == weight[:, None]) & (index[None, :] < index[:, None]))
    rank = jnp.sum(ahead.astype(jnp.int32), axis=1)
    rank = jnp.where(rank // CHIPS == 1, 3 * CHIPS - 1 - rank, rank)
    reach = jnp.sum(jnp.where(rank[None, :, None] == index[:, None, None], windows[None], 0), axis=1)
    far = (jnp.sum(windows[:, 1]) + CHIPS - 1) // CHIPS

    qh, kvh = pl.pallas_call(
        pack_kernel,
        out_shape=(
            jax.ShapeDtypeStruct((HEADS, PART, HD), jnp.bfloat16),
            jax.ShapeDtypeStruct((HEADS, 2, PART, HD), jnp.bfloat16),
        ),
        in_specs=[SMEM, VMEM, VMEM, VMEM],
        out_specs=(VMEM, VMEM),
        name="pack",
    )(rank, queries, keys, values)
    qh = qh.reshape(SLOTS, CHIPS, PART, HD)
    kvh = kvh.reshape(SLOTS, CHIPS, 2, PART, HD)

    def branch(n):
        def run(qh, kvh, reach):
            q, kv = gather(n, qh, kvh)
            return attend(reach, q, kv)

        return run

    o = lax.switch(far, [branch(n) for n in range(SLOTS + 1)], qh, kvh, reach)
    back = give_back(o)
    return pl.pallas_call(
        unpack_kernel,
        out_shape=jax.ShapeDtypeStruct((PART, HEADS * HD), jnp.bfloat16),
        in_specs=[SMEM, VMEM],
        out_specs=VMEM,
        name="unpack",
    )(rank, back.reshape(HEADS, PART, HD))


def solution(mesh):
    tokens = P(("slab", "head"), None)
    return jax.shard_map(
        shards, mesh=mesh, in_specs=(tokens, tokens, tokens, P()), out_specs=tokens, check_vma=False
    )
```

```python
import functools

import jax
import jax.numpy as jnp
from jax import lax
from jax.experimental import pallas as pl
from jax.experimental.pallas import tpu as pltpu
from jax.sharding import PartitionSpec as P

MESH = pl.DeviceIdType.MESH
ANY = pl.BlockSpec(memory_space=pl.ANY)
SMEM = pl.BlockSpec(memory_space=pltpu.SMEM)
VMEM = pl.BlockSpec(memory_space=pltpu.VMEM)
HEADS, HD, TILE, PART = 24, 128, 384, 96
SLOTS, CHIPS = 3, 8
LOG2E = 1.4426950408889634


def coords():
    slab, head = lax.axis_index("slab"), lax.axis_index("head")
    x, z, y_hi = slab // 16, (slab // 2) % 8, slab % 2
    return x, y_hi * 2 + head // 2, z, head % 2


def device(x, y, z, c):
    return ((x * 8 + z) * 2 + y // 2, (y % 2) * 2 + c)


def remote(src, dst, send, recv, to):
    return pltpu.make_async_remote_copy(
        src_ref=src, dst_ref=dst, send_sem=send, recv_sem=recv, device_id=to, device_id_type=MESH
    )


def greet(devices):
    barrier = pltpu.get_barrier_semaphore()
    for to in devices:
        pl.semaphore_signal(barrier, 1, device_id=to, device_id_type=MESH)
    pl.semaphore_wait(barrier, len(devices))


def group(x, y, z, c):
    return [
        device((x + 2 * i) % 4, (y + m) % 4, z, (c + n) % 2)
        for i in range(2)
        for m in range(4)
        for n in range(2)
        if (i, m, n) != (0, 0, 0)
    ]


def pack_kernel(perm, q_in, k_in, v_in, qh, kvh):
    for r in range(HEADS):
        cols = pl.ds(pl.multiple_of(perm[r] * HD, HD), HD)
        qh[r] = q_in[:, cols]
        kvh[r, 0] = k_in[:, cols]
        kvh[r, 1] = v_in[:, cols]


def pack(perm, queries, keys, values):
    qh, kvh = pl.pallas_call(
        pack_kernel,
        out_shape=(
            jax.ShapeDtypeStruct((HEADS, PART, HD), jnp.bfloat16),
            jax.ShapeDtypeStruct((HEADS, 2, PART, HD), jnp.bfloat16),
        ),
        in_specs=[SMEM, VMEM, VMEM, VMEM],
        out_specs=(VMEM, VMEM),
        name="pack",
    )(perm, queries, keys, values)
    return qh.reshape(SLOTS, CHIPS, PART, HD), kvh.reshape(SLOTS, CHIPS, 2, PART, HD)


def plan(far):
    main = [("begin", 0)]
    for k in range(far):
        for hop in range(2, 6):
            for part in range(2):
                main.append(("forward", k, hop, part))
            if k == 0 and hop == 2:
                main.append(("begin", 1))
            if k == 0 and hop == 5:
                main.append(("begin", 2))
            if k > 0 and hop == 2:
                main.append(("finish", k - 1))
            if k > 0 and hop == 4:
                main.append(("share", k - 1))
    if far == 0:
        main += [("begin", 1), ("begin", 2)]
    else:
        main += [("finish", far - 1), ("share", far - 1)]

    def ready(event):
        if event[0] == "begin":
            k = event[1]
            return [(0, k, "own"), (1, k, "inner")] + ([] if k < far else [(3, k, "outer")])
        if event[0] == "forward":
            k, hop, part = event[1:]
            if part == 1 and hop == 2:
                return [(0, k, "outer")]
            if part == 1 and hop == 5:
                return [(0, k, "near inner"), (1, k, "near own")]
            return []
        if event[0] == "finish":
            return [(0, event[1], "near outer")]
        return [(0, event[1], "side inner"), (1, event[1], "side own"), (4, event[1], "side outer")]

    steps, pool = [], []
    n = 0
    while n < len(main) or pool:
        events = []
        if n < len(main):
            events.append(main[n])
            pool += [(n + late, len(pool), k, what) for late, k, what in ready(main[n])]
        pool.sort(key=lambda p: p[0])
        pick = None
        if pool and (pool[0][0] <= n or n >= len(main)):
            pick = pool.pop(0)[2:]
        steps.append((events, pick))
        n += 1
    return steps


PLACES = ["own", "inner", "outer", "near own", "near inner", "near outer", "side own", "side inner", "side outer"]


def kernel(
    far, rank, barred, qh, kvh, out,
    q, kv, relay, vt, top, acc, o, back,
    a_send, q_send, kv_recv, q_recv, hop_send, hop_recv, own_send, own_recv,
    mid_send, mid_recv, x_send, x_recv, xs_send, xs_recv, o_send, o_recv,
):
    x, y, z, c = coords()
    z_hi, x_lo, t = z // 4, x % 2, x // 2
    up, down = (z + 1) % 8, (z + 7) % 8
    twin = device(x, y, z, 1 - c)
    side = device(x + 1 - 2 * x_lo, y, z, c)
    ahead = device(x, y, jnp.where(c == 0, up, down), c)
    first = device(x, y, jnp.where(c == 0, down, up), 1 - c)
    barrier = pltpu.get_barrier_semaphore()
    partners = group(x, y, z, c) + [
        device(x, y, up, c), device(x, y, up, 1 - c), device(x, y, down, c), device(x, y, down, 1 - c), side
    ]
    for to in partners:
        pl.semaphore_signal(barrier, 1, device_id=to, device_id_type=MESH)

    pl.semaphore_wait(barrier, len(partners))

    y_hi = y // 2
    part = (y % 2) * 2 + c
    me = t * 4 + y
    rows = pl.ds(part * PART, PART)
    copies = []

    def send(src, dst, sem, recv, chip):
        alone = (chip == me) & (c == y_hi)
        to = device((chip // 4) * 2 + x_lo, chip % 4, z, y_hi)

        @pl.when(alone)
        def _():
            pltpu.make_async_copy(src, dst, recv).start()

        @pl.when(jnp.logical_not(alone))
        def _():
            remote(src, dst, sem, recv, to).start()

        copies.append((alone, remote(src, dst, sem, recv, to)))

    def scatter(k):
        for i in range(CHIPS):
            chip = (me + i) % CHIPS
            send(kvh.at[k, chip], kv.at[k, 1, 1, :, t, rows], a_send.at[k, i], kv_recv.at[k], chip)

    scatter(0)
    for i in range(CHIPS):
        chip = (me + i) % CHIPS
        send(qh.at[:, chip], q.at[:, t, rows], q_send.at[i], q_recv, chip)
    scatter(1)
    scatter(2)
    top[...] = jnp.full_like(top, -1e30)
    acc[...] = jnp.zeros_like(acc)
    vt[HD:] = jnp.ones((16, 2 * TILE), jnp.bfloat16)

    outer = c * 2
    inner = 2 - outer
    near = 2 - 2 * z_hi
    z_next = jnp.where(c == 0, up, down)
    near_next = 2 - 2 * (z_next // 4)
    sender = x_lo == z_hi
    receiver = jnp.logical_not(sender)
    w_edge = jnp.where(c == 0, z % 4 > 0, z % 4 < 3)

    def wait_for(place, sem):
        pltpu.make_async_copy(place, place, sem).wait()

    def landing(k, hop, part, near_of):
        if hop == 1:
            return kv.at[k, 1, outer, part]
        if hop < 4:
            return relay.at[k, hop - 2, part]
        return kv.at[k, near_of, inner if hop == 4 else outer, part]

    def hop_wait(k, hop, part):
        wait_for(landing(k, hop, part, near), hop_recv.at[k, hop - 1, part])

    def first_hop(k, part):
        return remote(
            kv.at[k, 1, 1, part], kv.at[k, 1, inner, part], hop_send.at[k, 0, part], hop_recv.at[k, 0, part], first
        )

    def next_hop(k, hop, part):
        return remote(
            landing(k, hop - 1, part, near),
            landing(k, hop, part, near_next),
            hop_send.at[k, hop - 1, part],
            hop_recv.at[k, hop - 1, part],
            ahead,
        )

    def own_share(k):
        return remote(kv.at[k, 1, 1], kv.at[k, 1, outer], own_send.at[k], own_recv.at[k], twin)

    def mid_share(k):
        return remote(kv.at[k, near, inner], kv.at[k, near, 1], mid_send.at[k], mid_recv.at[k], twin)

    def aside(k, n):
        place = inner if n == 0 else outer
        return remote(kv.at[k, near, place], kv.at[k, 2 - near, place], x_send.at[k, n], x_recv.at[k, n], side)

    def side_share(k):
        return remote(kv.at[k, 2 - near, inner], kv.at[k, 2 - near, 1], xs_send.at[k], xs_recv.at[k], twin)

    def give_back(k, i):
        n = (t * 4 + part + i) % 8
        to = device((n // 4) * 2 + x_lo, c * 2 + (n % 4) // 2, z, n % 2)
        src = o.at[k, n // 4, pl.ds((n % 4) * PART, PART)]
        dst = back.at[k * CHIPS + me]
        return src, dst, remote(src, dst, o_send.at[k, i], o_recv.at[k], to)

    def communicate(event):
        what, k = event[0], event[1]
        if what == "begin":
            wait_for(kv.at[k, 1, 1], kv_recv.at[k])
            for part in range(2):
                first_hop(k, part).start()
            own_share(k).start()
            if k == 0:
                wait_for(q, q_recv)
        elif what == "forward":
            hop, part = event[2:]
            hop_wait(k, hop - 1, part)
            next_hop(k, hop, part).start()
            if hop == 5 and part == 1:
                mid_share(k).start()
                pl.when(sender)(aside(k, 0).start)
        elif what == "finish":
            for part in range(2):
                hop_wait(k, 5, part)
            pl.when(sender)(aside(k, 1).start)
        else:

            @pl.when(receiver)
            def _():
                wait_for(kv.at[k, 2 - near, inner], x_recv.at[k, 0])
                side_share(k).start()

    def arrive(k, what):
        if what == "inner":
            wait_for(kv.at[k, 1, inner], own_recv.at[k])
        elif what == "outer" and k >= far:
            for part in range(2):
                hop_wait(k, 1, part)
        elif what == "near own":
            wait_for(kv.at[k, near, 1], mid_recv.at[k])
        elif what == "side own":
            pl.when(receiver)(lambda: wait_for(kv.at[k, 2 - near, 1], xs_recv.at[k]))
        elif what == "side outer":
            pl.when(receiver)(lambda: wait_for(kv.at[k, 2 - near, outer], x_recv.at[k, 1]))

    scale = HD ** (-0.5) * LOG2E

    def attention(k, place):
        dh, dw = place // 3, place % 3
        row = k * CHIPS + me
        row_at = jnp.where(dh == 0, 1, jnp.where(dh == 1, near, 2 - near))
        col_at = jnp.where(dw == 0, 1, jnp.where(dw == 1, inner, outer))
        off = barred[row, 1] * jnp.minimum(dh, 1).astype(jnp.float32)
        off += barred[row, 2] * jnp.minimum(dw, 1).astype(jnp.float32)
        off += jnp.where((dw == 2) & jnp.logical_not(w_edge), 1e30, 0.0)
        off_time = off + barred[row, 0]
        tile = kv.at[k, row_at, col_at]
        vt[:HD] = tile[1].reshape(2 * TILE, HD).T
        scores = [
            [
                lax.dot_general(tile[0, u], q[k, s], (((1,), (1,)), ((), ())), preferred_element_type=jnp.float32)
                for u in range(2)
            ]
            for s in range(2)
        ]
        for s in range(2):
            old = top[k, s, :1]
            new = old
            for u in range(2):
                best = jnp.max(scores[s][u], axis=0, keepdims=True)
                new = jnp.maximum(new, best - (off if u == s else off_time))
            p = [
                jnp.exp2((scores[s][u] - (new + (off if u == s else off_time))) * scale).astype(jnp.bfloat16)
                for u in range(2)
            ]
            fix = jnp.exp2((old - new) * scale)
            add = jnp.dot(vt[...], jnp.concatenate(p, axis=0), preferred_element_type=jnp.float32)
            acc[k, s] = acc[k, s] * fix + add
            top[k, s] = jnp.broadcast_to(new, (8, TILE))

    def conclude(k):
        for s in range(2):
            o[k, s] = (acc[k, s, :HD] / acc[k, s, HD : HD + 1]).T.astype(jnp.bfloat16)
        for i in range(8):
            src, dst, copy = give_back(k, i)
            if i == 0:
                pl.when(y_hi == c)(pltpu.make_async_copy(src, dst, o_recv.at[k]).start)
                pl.when(y_hi != c)(copy.start)
            else:
                copy.start()

    steps = plan(far)
    last = {}
    for n, (events, pick) in enumerate(steps):
        if pick:
            last[pick[0]] = n

    def one_step(n, carry):
        code = jnp.int32(-1)
        for m, (events, pick) in enumerate(steps):

            @pl.when(n == m)
            def _():
                for event in events:
                    communicate(event)
                if pick:
                    arrive(*pick)

            if pick:
                code = jnp.where(n == m, pick[0] * 9 + PLACES.index(pick[1]), code)

        @pl.when((code >= 0) & ((code % 9 < 6) | receiver))
        def _():
            attention(code // 9, code % 9)

        for k in range(SLOTS):
            pl.when(n == last[k])(lambda: conclude(k))
        return carry

    lax.fori_loop(0, len(steps), one_step, 0)

    for k in range(SLOTS):
        wait_for(back.at[pl.ds(k * CHIPS, CHIPS)], o_recv.at[k])
    for e in range(HEADS):
        out[:, e * HD : (e + 1) * HD] = back[rank[e]]

    for alone, copy in copies:
        pl.when(jnp.logical_not(alone))(copy.wait_send)
    for k in range(SLOTS):
        for part_ in range(2):
            first_hop(k, part_).wait_send()
        own_share(k).wait_send()
        for i in range(8):
            copy = give_back(k, i)[2]
            if i == 0:
                pl.when(y_hi != c)(copy.wait_send)
            else:
                copy.wait_send()
    for k in range(far):
        for hop in range(2, 6):
            for part_ in range(2):
                next_hop(k, hop, part_).wait_send()
        mid_share(k).wait_send()
        for n in range(2):
            pl.when(sender)(aside(k, n).wait_send)
        pl.when(receiver)(side_share(k).wait_send)


def run(far, rank, barred, qh, kvh):
    dma = pltpu.SemaphoreType.DMA
    bf16, f32 = jnp.bfloat16, jnp.float32
    return pl.pallas_call(
        functools.partial(kernel, far),
        out_shape=jax.ShapeDtypeStruct((PART, HEADS * HD), bf16),
        in_specs=[SMEM, SMEM, ANY, ANY],
        out_specs=VMEM,
        scratch_shapes=[
            pltpu.VMEM((SLOTS, 2, TILE, HD), bf16),
            pltpu.VMEM((SLOTS, 3, 3, 2, 2, TILE, HD), bf16),
            pltpu.VMEM((SLOTS, 2, 2, 2, TILE, HD), bf16),
            pltpu.VMEM((HD + 16, 2 * TILE), bf16),
            pltpu.VMEM((SLOTS, 2, 8, TILE), f32),
            pltpu.VMEM((SLOTS, 2, HD + 16, TILE), f32),
            pltpu.VMEM((SLOTS, 2, TILE, HD), bf16),
            pltpu.VMEM((HEADS, PART, HD), bf16),
            dma((SLOTS, CHIPS)),
            dma((CHIPS,)),
            dma((SLOTS,)),
            dma,
            dma((SLOTS, 5, 2)),
            dma((SLOTS, 5, 2)),
            dma((SLOTS,)),
            dma((SLOTS,)),
            dma((SLOTS,)),
            dma((SLOTS,)),
            dma((SLOTS, 2)),
            dma((SLOTS, 2)),
            dma((SLOTS,)),
            dma((SLOTS,)),
            dma((SLOTS, 8)),
            dma((SLOTS,)),
        ],
        compiler_params=pltpu.CompilerParams(collective_id=far, has_side_effects=True, vmem_limit_bytes=48 << 20),
        name=f"tile_attention{far}",
    )(rank, barred, qh, kvh)


def shards(queries, keys, values, windows):
    weight = windows[:, 1] * 4 + windows[:, 2] * 2 + windows[:, 0]
    index = jnp.arange(HEADS, dtype=jnp.int32)
    ahead = (weight[None, :] > weight[:, None]) | ((weight[None, :] == weight[:, None]) & (index[None, :] < index[:, None]))
    rank = jnp.sum(ahead.astype(jnp.int32), axis=1)
    found = rank[None, :] == index[:, None]
    perm = jnp.sum(jnp.where(found, index[None], 0), axis=1)
    barred = jnp.sum(jnp.where(found[:, :, None] & (windows[None] < 1), jnp.float32(1e30), 0.0), axis=1)
    far = (jnp.sum(windows[:, 1]) + CHIPS - 1) // CHIPS
    qh, kvh = pack(perm, queries, keys, values)
    return lax.switch(far, [functools.partial(run, n) for n in range(SLOTS + 1)], rank, barred, qh, kvh)


def solution(mesh):
    tokens = P(("slab", "head"), None)
    return jax.shard_map(
        shards, mesh=mesh, in_specs=(tokens, tokens, tokens, P()), out_specs=tokens, check_vma=False
    )
```

```python
import functools

import jax
import jax.numpy as jnp
from jax import lax
from jax.experimental import pallas as pl
from jax.experimental.pallas import tpu as pltpu
from jax.sharding import PartitionSpec as P

MESH = pl.DeviceIdType.MESH
ANY = pl.BlockSpec(memory_space=pl.ANY)
SMEM = pl.BlockSpec(memory_space=pltpu.SMEM)
VMEM = pl.BlockSpec(memory_space=pltpu.VMEM)
HEADS, HD, TILE, PART = 24, 128, 384, 96
SLOTS, CHIPS = 3, 8
LOG2E = 1.4426950408889634


def coords():
    slab, head = lax.axis_index("slab"), lax.axis_index("head")
    x, z, y_hi = slab // 16, (slab // 2) % 8, slab % 2
    return x, y_hi * 2 + head // 2, z, head % 2


def device(x, y, z, c):
    return ((x * 8 + z) * 2 + y // 2, (y % 2) * 2 + c)


def remote(src, dst, send, recv, to):
    return pltpu.make_async_remote_copy(
        src_ref=src, dst_ref=dst, send_sem=send, recv_sem=recv, device_id=to, device_id_type=MESH
    )


def greet(devices):
    barrier = pltpu.get_barrier_semaphore()
    for to in devices:
        pl.semaphore_signal(barrier, 1, device_id=to, device_id_type=MESH)
    pl.semaphore_wait(barrier, len(devices))


def group(x, y, z, c):
    return [
        device((x + 2 * i) % 4, (y + m) % 4, z, (c + n) % 2)
        for i in range(2)
        for m in range(4)
        for n in range(2)
        if (i, m, n) != (0, 0, 0)
    ]


def pack_kernel(windows, q_in, k_in, v_in, qh, kvh, rank, barred, form):
    key = [windows[e, 1] * 4 + windows[e, 2] * 2 + windows[e, 0] for e in range(HEADS)]
    place = [jnp.int32(0)] * HEADS
    for e in range(HEADS):
        for f in range(e):
            first = (key[f] >= key[e]).astype(jnp.int32)
            place[e] += first
            place[f] += 1 - first
    tall = both = jnp.int32(0)
    for e in range(HEADS):
        r = place[e]
        cols = pl.ds(e * HD, HD)
        qh[r] = q_in[:, cols]
        kvh[r, 0] = k_in[:, cols]
        kvh[r, 1] = v_in[:, cols]
        rank[e] = r
        tall += windows[e, 1]
        both += windows[e, 1] * windows[e, 2]
        for axis in range(3):
            barred[r, axis] = jnp.where(windows[e, axis] > 0, 0.0, 1e30).astype(jnp.float32)
    far = (tall + CHIPS - 1) // CHIPS
    form[0] = jnp.where(far == 0, 0, 2 * far - 1 + (both > CHIPS * (far - 1)).astype(jnp.int32))


def pack(windows, queries, keys, values):
    qh, kvh, rank, barred, form = pl.pallas_call(
        pack_kernel,
        out_shape=(
            jax.ShapeDtypeStruct((HEADS, PART, HD), jnp.bfloat16),
            jax.ShapeDtypeStruct((HEADS, 2, PART, HD), jnp.bfloat16),
            jax.ShapeDtypeStruct((HEADS,), jnp.int32),
            jax.ShapeDtypeStruct((HEADS, 3), jnp.float32),
            jax.ShapeDtypeStruct((1,), jnp.int32),
        ),
        in_specs=[SMEM, VMEM, VMEM, VMEM],
        out_specs=(VMEM, VMEM, SMEM, SMEM, SMEM),
        name="pack",
    )(windows, queries, keys, values)
    return form[0], rank, barred, qh.reshape(SLOTS, CHIPS, PART, HD), kvh.reshape(SLOTS, CHIPS, 2, PART, HD)


def plan(far, wide):
    main = [("begin", 0)]
    for k in range(far):
        for hop in range(2, 6):
            for part in range(2):
                main.append(("forward" if hop < 5 else "near", k, hop, part))
            if k == 0 and hop == 3:
                main.append(("begin", 1))
            if (k, hop) == ((1, 3) if far == 3 else (far - 1, 4)):
                main.append(("begin", 2))
            if k > 0 and hop == 2 and k - 1 < wide:
                main.append(("finish", k - 1))
            if k > 0 and hop == 4:
                main += [("share", k - 1, 0), ("share", k - 1, 1)]
    if far == 0:
        main += [("begin", 1), ("begin", 2)]
    else:
        main += [("finish", far - 1) if far <= wide else None, None, None, ("share", far - 1, 0), ("share", far - 1, 1)]

    def ready(event):
        what, k = event[0], event[1]
        if what == "begin" and k == 1:
            return [(0, 0, "own"), (0, 0, "inner"), (0, 0, "outer"), (0, 1, "own"), (0, 1, "inner")] + (
                [] if far > 1 else [(3, 1, "outer")]
            )
        if what == "begin" and k == 2:
            return [(0, 2, "own"), (1, 2, "inner")] + ([] if far > 2 else [(3, 2, "outer")])
        if what == "forward" and event[2:] == (2, 1) and k > 0:
            return [(0, k, "outer")]
        if what == "near" and event[3] == 1:
            return [(0, k, "near inner"), (1, k, "near own")]
        if what == "finish":
            return [(0, k, "near outer")]
        if what == "share" and event[2] == 1:
            return [(0, k, "side inner"), (1, k, "side own")] + ([(3, k, "side outer")] if k < wide else [])
        return []

    steps, pool = [], []
    n = 0
    while n < len(main) or pool:
        events = []
        if n < len(main) and main[n]:
            events.append(main[n])
            pool += [(n + late, len(pool), k, what) for late, k, what in ready(main[n])]
        pool.sort(key=lambda p: p[0])
        pick = None
        if pool and (pool[0][0] <= n or n >= len(main)):
            pick = pool.pop(0)[2:]
        steps.append((events, pick))
        n += 1
    return steps


PLACES = ["own", "inner", "outer", "near own", "near inner", "near outer", "side own", "side inner", "side outer"]


def kernel(
    far, wide, rank, barred, qh, kvh, out,
    q, kv, relay, vt, top, acc, o, back,
    a_send, q_send, kv_recv, q_recv, hop_send, hop_recv, own_send, own_recv,
    mid_send, mid_recv, x_send, x_recv, xs_send, xs_recv, halo_send, halo_recv, o_send, o_recv,
):
    x, y, z, c = coords()
    z_hi, x_lo, t = z // 4, x % 2, x // 2
    up, down = (z + 1) % 8, (z + 7) % 8
    twin = device(x, y, z, 1 - c)
    side = device(x + 1 - 2 * x_lo, y, z, c)
    ahead = device(x, y, jnp.where(c == 0, up, down), c)
    first = device(x, y, jnp.where(c == 0, down, up), 1 - c)
    barrier = pltpu.get_barrier_semaphore()
    partners = group(x, y, z, c) + [
        device(x, y, up, c), device(x, y, up, 1 - c), device(x, y, down, c), device(x, y, down, 1 - c), side
    ]
    for to in partners:
        pl.semaphore_signal(barrier, 1, device_id=to, device_id_type=MESH)

    pl.semaphore_wait(barrier, len(partners))

    y_hi = y // 2
    part = (y % 2) * 2 + c
    me = t * 4 + y
    rows = pl.ds(part * PART, PART)
    def spread(act):
        def one(i, src, dst, sem, recv, chip):
            copy = remote(src, dst, sem, recv, device((chip // 4) * 2 + x_lo, chip % 4, z, y_hi))
            if i > 0:
                act(copy)
            else:
                pl.when(c != y_hi)(lambda: act(copy))
                if act is start:
                    pl.when(c == y_hi)(pltpu.make_async_copy(src, dst, recv).start)

        return one

    def start(copy):
        copy.start()

    def sent(copy):
        copy.wait_send()

    def scatter(k, act):
        for p in range(2):
            for i in range(CHIPS):
                chip = (me + i) % CHIPS
                spread(act)(i, kvh.at[k, chip, p], kv.at[k, 1, 1, p, t, rows], a_send.at[k, p, i], kv_recv.at[k, p], chip)

    def scatter_queries(act):
        for i in range(CHIPS):
            chip = (me + i) % CHIPS
            spread(act)(i, qh.at[:, chip], q.at[:, t, rows], q_send.at[i], q_recv, chip)

    scatter(0, start)
    top[...] = jnp.full_like(top, -1e30)
    acc[...] = jnp.zeros_like(acc)
    vt[HD:] = jnp.ones((16, 2 * TILE), jnp.bfloat16)

    outer = c * 2
    inner = 2 - outer
    near = 2 - 2 * z_hi
    z_next = jnp.where(c == 0, up, down)
    near_next = 2 - 2 * (z_next // 4)
    sender = x_lo == z_hi
    receiver = jnp.logical_not(sender)
    w_edge = jnp.where(c == 0, z % 4 > 0, z % 4 < 3)
    halo_to = receiver & jnp.where(c == 0, z % 4 < 3, z % 4 > 0)
    halo_from = receiver & w_edge

    def wait_for(place, sem):
        pltpu.make_async_copy(place, place, sem).wait()

    def landing(k, hop, part, near_of):
        if hop == 1:
            return kv.at[k, 1, outer, part]
        if hop < 4:
            return relay.at[k, hop - 2, part]
        return kv.at[k, near_of, inner if hop == 4 else outer, part]

    def hop_wait(k, hop, part):
        wait_for(landing(k, hop, part, near), hop_recv.at[k, hop - 1, part])

    def first_hop(k, part):
        return remote(
            kv.at[k, 1, 1, part], kv.at[k, 1, inner, part], hop_send.at[k, 0, part], hop_recv.at[k, 0, part], first
        )

    def next_hop(k, hop, part):
        return remote(
            landing(k, hop - 1, part, near),
            landing(k, hop, part, near_next),
            hop_send.at[k, hop - 1, part],
            hop_recv.at[k, hop - 1, part],
            ahead,
        )

    def own_share(k):
        return remote(kv.at[k, 1, 1], kv.at[k, 1, outer], own_send.at[k], own_recv.at[k], twin)

    def mid_share(k):
        return remote(kv.at[k, near, inner], kv.at[k, near, 1], mid_send.at[k], mid_recv.at[k], twin)

    def aside(k, n, part):
        place = inner if n == 0 else outer
        return remote(
            kv.at[k, near, place, part], kv.at[k, 2 - near, place, part], x_send.at[k, n, part], x_recv.at[k, n, part], side
        )

    def side_wait(k, n, part):
        wait_for(kv.at[k, 2 - near, inner if n == 0 else outer, part], x_recv.at[k, n, part])

    def side_share(k, part):
        place = kv.at[k, 2 - near, inner, part]
        return remote(place, kv.at[k, 2 - near, 1, part], xs_send.at[k, part], xs_recv.at[k, part], twin)

    def halo(k, part):
        place = kv.at[k, 2 - near, inner, part]
        return remote(place, kv.at[k, 2 - near, outer, part], halo_send.at[part], halo_recv.at[part], ahead)

    def give_back(k, i):
        n = (t * 4 + part + i) % 8
        to = device((n // 4) * 2 + x_lo, c * 2 + (n % 4) // 2, z, n % 2)
        src = o.at[k, n // 4, pl.ds((n % 4) * PART, PART)]
        dst = back.at[k * CHIPS + me]
        return src, dst, remote(src, dst, o_send.at[k, i], o_recv.at[k], to)

    def communicate(event):
        what, k = event[0], event[1]
        if what == "begin":
            for part in range(2):
                wait_for(kv.at[k, 1, 1, part], kv_recv.at[k, part])
                first_hop(k, part).start()
            own_share(k).start()
            if k == 0:
                scatter_queries(start)
                scatter(1, start)
            if k == 1:
                wait_for(q, q_recv)
                scatter(2, start)
        elif what == "forward":
            hop, part = event[2:]
            hop_wait(k, hop - 1, part)
            next_hop(k, hop, part).start()
        elif what == "near":
            part = event[3]
            hop_wait(k, 4, part)
            if k < wide:
                next_hop(k, 5, part).start()
            pl.when(sender)(aside(k, 0, part).start)
            if part == 1:
                mid_share(k).start()
        elif what == "finish":
            for part in range(2):
                hop_wait(k, 5, part)
                if k < far - 1:
                    pl.when(sender)(aside(k, 1, part).start)
        else:
            part = event[2]

            @pl.when(receiver)
            def _():
                side_wait(k, 0, part)
                side_share(k, part).start()

            if k == far - 1 and k < wide:
                pl.when(halo_to)(halo(k, part).start)

    def arrive(k, what):
        if what == "inner":
            wait_for(kv.at[k, 1, inner], own_recv.at[k])
        elif what == "outer" and k >= far:
            for part in range(2):
                hop_wait(k, 1, part)
        elif what == "near own":
            wait_for(kv.at[k, near, 1], mid_recv.at[k])
        elif what == "side own":

            @pl.when(receiver)
            def _():
                for part in range(2):
                    wait_for(kv.at[k, 2 - near, 1, part], xs_recv.at[k, part])

        elif what == "side outer":

            @pl.when(halo_from if k == far - 1 else receiver)
            def _():
                for part in range(2):
                    if k == far - 1:
                        wait_for(kv.at[k, 2 - near, outer, part], halo_recv.at[part])
                    else:
                        side_wait(k, 1, part)

    scale = HD ** (-0.5) * LOG2E

    def attention(k, place):
        dh, dw = place // 3, place % 3
        row = k * CHIPS + me
        row_at = jnp.where(dh == 0, 1, jnp.where(dh == 1, near, 2 - near))
        col_at = jnp.where(dw == 0, 1, jnp.where(dw == 1, inner, outer))
        off = barred[row, 1] * jnp.minimum(dh, 1).astype(jnp.float32)
        off += barred[row, 2] * jnp.minimum(dw, 1).astype(jnp.float32)
        off += jnp.where((dw == 2) & jnp.logical_not(w_edge), 1e30, 0.0)
        off_time = off + barred[row, 0]
        tile = kv.at[k, row_at, col_at]
        vt[:HD] = tile[1].reshape(2 * TILE, HD).T
        scores = [
            [
                lax.dot_general(tile[0, u], q[k, s], (((1,), (1,)), ((), ())), preferred_element_type=jnp.float32)
                for u in range(2)
            ]
            for s in range(2)
        ]
        for s in range(2):
            old = top[k, s, :1]
            new = old
            for u in range(2):
                best = jnp.max(scores[s][u], axis=0, keepdims=True)
                new = jnp.maximum(new, best - (off if u == s else off_time))
            p = [
                jnp.exp2((scores[s][u] - (new + (off if u == s else off_time))) * scale).astype(jnp.bfloat16)
                for u in range(2)
            ]
            fix = jnp.exp2((old - new) * scale)
            add = jnp.dot(vt[...], jnp.concatenate(p, axis=0), preferred_element_type=jnp.float32)
            acc[k, s] = acc[k, s] * fix + add
            top[k, s] = jnp.broadcast_to(new, (8, TILE))

    def conclude(k):
        for s in range(2):
            o[k, s] = (acc[k, s, :HD] / acc[k, s, HD : HD + 1]).T.astype(jnp.bfloat16)
        for i in range(8):
            src, dst, copy = give_back(k, i)
            if i == 0:
                pl.when(y_hi == c)(pltpu.make_async_copy(src, dst, o_recv.at[k]).start)
                pl.when(y_hi != c)(copy.start)
            else:
                copy.start()

    steps = plan(far, wide)
    last = {}
    for n, (events, pick) in enumerate(steps):
        if pick:
            last[pick[0]] = n

    def one_step(n, carry):
        code = jnp.int32(-1)
        for m, (events, pick) in enumerate(steps):

            @pl.when(n == m)
            def _():
                for event in events:
                    communicate(event)
                if pick:
                    arrive(*pick)

            if pick:
                code = jnp.where(n == m, pick[0] * 9 + PLACES.index(pick[1]), code)

        @pl.when((code >= 0) & ((code % 9 < 6) | receiver) & ((code % 9 != 8) | halo_from))
        def _():
            attention(code // 9, code % 9)

        for k in range(SLOTS):
            pl.when(n == last[k])(lambda: conclude(k))
        return carry

    lax.fori_loop(0, len(steps), one_step, 0)

    for k in range(SLOTS):
        wait_for(back.at[pl.ds(k * CHIPS, CHIPS)], o_recv.at[k])
    for e in range(HEADS):
        out[:, e * HD : (e + 1) * HD] = back[rank[e]]

    scatter_queries(sent)
    for k in range(SLOTS):
        scatter(k, sent)
        for part_ in range(2):
            first_hop(k, part_).wait_send()
        own_share(k).wait_send()
        for i in range(8):
            copy = give_back(k, i)[2]
            if i == 0:
                pl.when(y_hi != c)(copy.wait_send)
            else:
                copy.wait_send()
    for k in range(far):
        for hop in range(2, 6 if k < wide else 5):
            for part_ in range(2):
                next_hop(k, hop, part_).wait_send()
        mid_share(k).wait_send()
        for part_ in range(2):
            for n in range(2 if k < min(wide, far - 1) else 1):
                pl.when(sender)(aside(k, n, part_).wait_send)
            pl.when(receiver)(side_share(k, part_).wait_send)
            if k == far - 1 and k < wide:
                pl.when(halo_to)(halo(k, part_).wait_send)


def run(far, wide, rank, barred, qh, kvh):
    dma = pltpu.SemaphoreType.DMA
    bf16, f32 = jnp.bfloat16, jnp.float32
    return pl.pallas_call(
        functools.partial(kernel, far, wide),
        out_shape=jax.ShapeDtypeStruct((PART, HEADS * HD), bf16),
        in_specs=[SMEM, SMEM, ANY, ANY],
        out_specs=VMEM,
        scratch_shapes=[
            pltpu.VMEM((SLOTS, 2, TILE, HD), bf16),
            pltpu.VMEM((SLOTS, 3, 3, 2, 2, TILE, HD), bf16),
            pltpu.VMEM((SLOTS, 2, 2, 2, TILE, HD), bf16),
            pltpu.VMEM((HD + 16, 2 * TILE), bf16),
            pltpu.VMEM((SLOTS, 2, 8, TILE), f32),
            pltpu.VMEM((SLOTS, 2, HD + 16, TILE), f32),
            pltpu.VMEM((SLOTS, 2, TILE, HD), bf16),
            pltpu.VMEM((HEADS, PART, HD), bf16),
            dma((SLOTS, 2, CHIPS)),
            dma((CHIPS,)),
            dma((SLOTS, 2)),
            dma,
            dma((SLOTS, 5, 2)),
            dma((SLOTS, 5, 2)),
            dma((SLOTS,)),
            dma((SLOTS,)),
            dma((SLOTS,)),
            dma((SLOTS,)),
            dma((SLOTS, 2, 2)),
            dma((SLOTS, 2, 2)),
            dma((SLOTS, 2)),
            dma((SLOTS, 2)),
            dma((2,)),
            dma((2,)),
            dma((SLOTS, 8)),
            dma((SLOTS,)),
        ],
        compiler_params=pltpu.CompilerParams(collective_id=far * 4 + wide, has_side_effects=True, vmem_limit_bytes=48 << 20),
        name=f"tile_attention{far}{wide}",
    )(rank, barred, qh, kvh)


def shards(queries, keys, values, windows):
    form, rank, barred, qh, kvh = pack(windows, queries, keys, values)
    forms = [(0, 0), (1, 0), (1, 1), (2, 1), (2, 2), (3, 2), (3, 3)]
    return lax.switch(form, [functools.partial(run, *f) for f in forms], rank, barred, qh, kvh)


def solution(mesh):
    tokens = P(("slab", "head"), None)
    return jax.shard_map(
        shards, mesh=mesh, in_specs=(tokens, tokens, tokens, P()), out_specs=tokens, check_vma=False
    )
```

```python
import functools

import jax
import jax.numpy as jnp
from jax import lax
from jax.experimental import pallas as pl
from jax.experimental.pallas import tpu as pltpu
from jax.sharding import PartitionSpec as P

MESH = pl.DeviceIdType.MESH
ANY = pl.BlockSpec(memory_space=pl.ANY)
SMEM = pl.BlockSpec(memory_space=pltpu.SMEM)
VMEM = pl.BlockSpec(memory_space=pltpu.VMEM)
HEADS, HD, TILE, PART = 24, 128, 384, 96
SLOTS, CHIPS = 3, 8
LOG2E = 1.4426950408889634


def coords():
    slab, head = lax.axis_index("slab"), lax.axis_index("head")
    x, z, y_hi = slab // 16, (slab // 2) % 8, slab % 2
    return x, y_hi * 2 + head // 2, z, head % 2


def device(x, y, z, c):
    return ((x * 8 + z) * 2 + y // 2, (y % 2) * 2 + c)


def remote(src, dst, send, recv, to):
    return pltpu.make_async_remote_copy(
        src_ref=src, dst_ref=dst, send_sem=send, recv_sem=recv, device_id=to, device_id_type=MESH
    )


def greet(devices):
    barrier = pltpu.get_barrier_semaphore()
    for to in devices:
        pl.semaphore_signal(barrier, 1, device_id=to, device_id_type=MESH)
    pl.semaphore_wait(barrier, len(devices))


def group(x, y, z, c):
    return [
        device((x + 2 * i) % 4, (y + m) % 4, z, (c + n) % 2)
        for i in range(2)
        for m in range(4)
        for n in range(2)
        if (i, m, n) != (0, 0, 0)
    ]


def pack_kernel(windows, q_hbm, k_hbm, v_hbm, qh, kvh, rank, barred, form, q_in, k_in, v_in, sem):
    loads = [
        pltpu.make_async_copy(src, dst, sem.at[i])
        for i, (src, dst) in enumerate([(k_hbm, k_in), (v_hbm, v_in), (q_hbm, q_in)])
    ]
    for load in loads:
        load.start()
    key = [windows[e, 1] * 4 + windows[e, 2] * 2 + windows[e, 0] for e in range(HEADS)]
    place = [jnp.int32(0)] * HEADS
    for e in range(HEADS):
        for f in range(e):
            first = (key[f] >= key[e]).astype(jnp.int32)
            place[e] += first
            place[f] += 1 - first
    tall = both = jnp.int32(0)
    for e in range(HEADS):
        r = place[e]
        rank[e] = r
        tall += windows[e, 1]
        both += windows[e, 1] * windows[e, 2]
        for axis in range(3):
            barred[r, axis] = jnp.where(windows[e, axis] > 0, 0.0, 1e30).astype(jnp.float32)
    far = (tall + CHIPS - 1) // CHIPS
    form[0] = jnp.where(far == 0, 0, 2 * far - 1 + (both > CHIPS * (far - 1)).astype(jnp.int32))
    for load in loads:
        load.wait()
    for e in range(HEADS):
        r = place[e]
        cols = pl.ds(e * HD, HD)
        qh[r] = q_in[:, cols]
        kvh[r, 0] = k_in[:, cols]
        kvh[r, 1] = v_in[:, cols]


def pack(windows, queries, keys, values):
    qh, kvh, rank, barred, form = pl.pallas_call(
        pack_kernel,
        out_shape=(
            jax.ShapeDtypeStruct((HEADS, PART, HD), jnp.bfloat16),
            jax.ShapeDtypeStruct((HEADS, 2, PART, HD), jnp.bfloat16),
            jax.ShapeDtypeStruct((HEADS,), jnp.int32),
            jax.ShapeDtypeStruct((HEADS, 3), jnp.float32),
            jax.ShapeDtypeStruct((1,), jnp.int32),
        ),
        in_specs=[SMEM, ANY, ANY, ANY],
        out_specs=(VMEM, VMEM, SMEM, SMEM, SMEM),
        scratch_shapes=[pltpu.VMEM((PART, HEADS * HD), jnp.bfloat16)] * 3 + [pltpu.SemaphoreType.DMA((3,))],
        name="pack",
    )(windows, queries, keys, values)
    return form[0], rank, barred, qh.reshape(SLOTS, CHIPS, PART, HD), kvh.reshape(SLOTS, CHIPS, 2, PART, HD)


def plan(far, wide):
    def hops(k, hop):
        return [("forward" if hop < 5 else "near", k, hop, part) for part in range(2)]

    if far == 0:
        main = [("begin", 0), ("ask", 0), ("begin", 1), ("queries", 0), ("begin", 2)]
    else:
        main = [("begin", 0)] + hops(0, 2) + [("ask", 0)] + hops(0, 3) + [("begin", 1)] + hops(0, 4) + [("queries", 0)]
        if far == 1:
            main.append(("begin", 2))
        for k in range(1, far):
            main += hops(k, 2) + hops(k - 1, 5) + hops(k, 3)
            if (far, k) == (3, 1):
                main.append(("begin", 2))
            if k - 1 < wide:
                main.append(("finish", k - 1))
            main += hops(k, 4)
            if far == 2:
                main.append(("begin", 2))
            main += [("share", k - 1, 0), ("share", k - 1, 1)]
        main += hops(far - 1, 5) + [("finish", far - 1) if far <= wide else None, None, None]
        main += [("share", far - 1, 0), ("share", far - 1, 1)]

    def ready(event):
        what, k = event[0], event[1]
        if what == "queries":
            return [(0, 0, "own"), (0, 0, "inner"), (0, 0, "outer"), (0, 1, "own"), (0, 1, "inner")] + (
                [] if far > 1 else [(3, 1, "outer")]
            )
        if what == "begin" and k == 2:
            return [(0, 2, "own"), (1, 2, "inner")] + ([] if far > 2 else [(3, 2, "outer")])
        if what == "forward" and event[2:] == (2, 1) and k > 0:
            return [(0, k, "outer")]
        if what == "near" and event[3] == 1:
            return [(0, k, "near inner"), (1, k, "near own")]
        if what == "finish":
            return [(0, k, "near outer")]
        if what == "share" and event[2] == 1:
            return [(0, k, "side inner"), (1, k, "side own")] + ([(3, k, "side outer")] if k < wide else [])
        return []

    steps, pool = [], []
    n = 0
    while n < len(main) or pool:
        events = []
        if n < len(main) and main[n]:
            events.append(main[n])
            pool += [(n + late, len(pool), k, what) for late, k, what in ready(main[n])]
        pool.sort(key=lambda p: p[0])
        pick = None
        if pool and (pool[0][0] <= n or n >= len(main)):
            pick = pool.pop(0)[2:]
        steps.append((events, pick))
        n += 1
    return steps


PLACES = ["own", "inner", "outer", "near own", "near inner", "near outer", "side own", "side inner", "side outer"]


def kernel(
    far, wide, rank, barred, qh, kvh, out,
    q, kv, relay, vt, top, acc, o, back,
    a_send, q_send, kv_recv, q_recv, hop_send, hop_recv, own_send, own_recv,
    mid_send, mid_recv, x_send, x_recv, xs_send, xs_recv, halo_send, halo_recv, o_send, o_recv,
):
    x, y, z, c = coords()
    z_hi, x_lo, t = z // 4, x % 2, x // 2
    up, down = (z + 1) % 8, (z + 7) % 8
    twin = device(x, y, z, 1 - c)
    side = device(x + 1 - 2 * x_lo, y, z, c)
    ahead = device(x, y, jnp.where(c == 0, up, down), c)
    first = device(x, y, jnp.where(c == 0, down, up), 1 - c)
    barrier = pltpu.get_barrier_semaphore()
    partners = group(x, y, z, c) + [
        device(x, y, up, c), device(x, y, up, 1 - c), device(x, y, down, c), device(x, y, down, 1 - c), side
    ]
    for to in partners:
        pl.semaphore_signal(barrier, 1, device_id=to, device_id_type=MESH)

    pl.semaphore_wait(barrier, len(partners))

    y_hi = y // 2
    part = (y % 2) * 2 + c
    me = t * 4 + y
    rows = pl.ds(part * PART, PART)
    def spread(act):
        def one(i, src, dst, sem, recv, chip):
            copy = remote(src, dst, sem, recv, device((chip // 4) * 2 + x_lo, chip % 4, z, y_hi))
            if i > 0:
                act(copy)
            else:
                pl.when(c != y_hi)(lambda: act(copy))
                if act is start:
                    pl.when(c == y_hi)(pltpu.make_async_copy(src, dst, recv).start)

        return one

    def start(copy):
        copy.start()

    def sent(copy):
        copy.wait_send()

    def scatter(k, act):
        for p in range(2):
            for i in range(CHIPS):
                chip = (me + i) % CHIPS
                spread(act)(i, kvh.at[k, chip, p], kv.at[k, 1, 1, p, t, rows], a_send.at[k, p, i], kv_recv.at[k, p], chip)

    def scatter_queries(act):
        for i in range(CHIPS):
            chip = (me + i) % CHIPS
            spread(act)(i, qh.at[:, chip], q.at[:, t, rows], q_send.at[i], q_recv, chip)

    scatter(0, start)
    top[...] = jnp.full_like(top, -1e30)
    acc[...] = jnp.zeros_like(acc)
    vt[HD:] = jnp.ones((16, 2 * TILE), jnp.bfloat16)

    outer = c * 2
    inner = 2 - outer
    near = 2 - 2 * z_hi
    z_next = jnp.where(c == 0, up, down)
    near_next = 2 - 2 * (z_next // 4)
    sender = x_lo == z_hi
    receiver = jnp.logical_not(sender)
    w_edge = jnp.where(c == 0, z % 4 > 0, z % 4 < 3)
    halo_to = receiver & jnp.where(c == 0, z % 4 < 3, z % 4 > 0)
    halo_from = receiver & w_edge

    def wait_for(place, sem):
        pltpu.make_async_copy(place, place, sem).wait()

    def landing(k, hop, part, near_of):
        if hop == 1:
            return kv.at[k, 1, outer, part]
        if hop < 4:
            return relay.at[k, hop - 2, part]
        return kv.at[k, near_of, inner if hop == 4 else outer, part]

    def hop_wait(k, hop, part):
        wait_for(landing(k, hop, part, near), hop_recv.at[k, hop - 1, part])

    def first_hop(k, part):
        return remote(
            kv.at[k, 1, 1, part], kv.at[k, 1, inner, part], hop_send.at[k, 0, part], hop_recv.at[k, 0, part], first
        )

    def next_hop(k, hop, part):
        return remote(
            landing(k, hop - 1, part, near),
            landing(k, hop, part, near_next),
            hop_send.at[k, hop - 1, part],
            hop_recv.at[k, hop - 1, part],
            ahead,
        )

    def own_share(k):
        return remote(kv.at[k, 1, 1], kv.at[k, 1, outer], own_send.at[k], own_recv.at[k], twin)

    def mid_share(k):
        return remote(kv.at[k, near, inner], kv.at[k, near, 1], mid_send.at[k], mid_recv.at[k], twin)

    def aside(k, n, part):
        place = inner if n == 0 else outer
        return remote(
            kv.at[k, near, place, part], kv.at[k, 2 - near, place, part], x_send.at[k, n, part], x_recv.at[k, n, part], side
        )

    def side_wait(k, n, part):
        wait_for(kv.at[k, 2 - near, inner if n == 0 else outer, part], x_recv.at[k, n, part])

    def side_share(k, part):
        place = kv.at[k, 2 - near, inner, part]
        return remote(place, kv.at[k, 2 - near, 1, part], xs_send.at[k, part], xs_recv.at[k, part], twin)

    def halo(k, part):
        place = kv.at[k, 2 - near, inner, part]
        return remote(place, kv.at[k, 2 - near, outer, part], halo_send.at[part], halo_recv.at[part], ahead)

    def give_back(k, i):
        n = (t * 4 + part + i) % 8
        to = device((n // 4) * 2 + x_lo, c * 2 + (n % 4) // 2, z, n % 2)
        src = o.at[k, n // 4, pl.ds((n % 4) * PART, PART)]
        dst = back.at[k * CHIPS + me]
        return src, dst, remote(src, dst, o_send.at[k, i], o_recv.at[k], to)

    def communicate(event):
        what, k = event[0], event[1]
        if what == "begin":
            for part in range(2):
                wait_for(kv.at[k, 1, 1, part], kv_recv.at[k, part])
                first_hop(k, part).start()
            own_share(k).start()
            if k < 2:
                scatter(k + 1, start)
        elif what == "ask":
            scatter_queries(start)
        elif what == "queries":
            wait_for(q, q_recv)
        elif what == "forward":
            hop, part = event[2:]
            hop_wait(k, hop - 1, part)
            next_hop(k, hop, part).start()
        elif what == "near":
            part = event[3]
            hop_wait(k, 4, part)
            if k < wide:
                next_hop(k, 5, part).start()
            pl.when(sender)(aside(k, 0, part).start)
            if part == 1:
                mid_share(k).start()
        elif what == "finish":
            for part in range(2):
                hop_wait(k, 5, part)
                if k < far - 1:
                    pl.when(sender)(aside(k, 1, part).start)
        else:
            part = event[2]

            @pl.when(receiver)
            def _():
                side_wait(k, 0, part)
                side_share(k, part).start()

            if k == far - 1 and k < wide:
                pl.when(halo_to)(halo(k, part).start)

    def arrive(k, what):
        if what == "inner":
            wait_for(kv.at[k, 1, inner], own_recv.at[k])
        elif what == "outer" and k >= far:
            for part in range(2):
                hop_wait(k, 1, part)
        elif what == "near own":
            wait_for(kv.at[k, near, 1], mid_recv.at[k])
        elif what == "side own":

            @pl.when(receiver)
            def _():
                for part in range(2):
                    wait_for(kv.at[k, 2 - near, 1, part], xs_recv.at[k, part])

        elif what == "side outer":

            @pl.when(halo_from if k == far - 1 else receiver)
            def _():
                for part in range(2):
                    if k == far - 1:
                        wait_for(kv.at[k, 2 - near, outer, part], halo_recv.at[part])
                    else:
                        side_wait(k, 1, part)

    scale = HD ** (-0.5) * LOG2E

    def attention(k, place):
        dh, dw = place // 3, place % 3
        row = k * CHIPS + me
        row_at = jnp.where(dh == 0, 1, jnp.where(dh == 1, near, 2 - near))
        col_at = jnp.where(dw == 0, 1, jnp.where(dw == 1, inner, outer))
        off = barred[row, 1] * jnp.minimum(dh, 1).astype(jnp.float32)
        off += barred[row, 2] * jnp.minimum(dw, 1).astype(jnp.float32)
        off += jnp.where((dw == 2) & jnp.logical_not(w_edge), 1e30, 0.0)
        off_time = off + barred[row, 0]
        tile = kv.at[k, row_at, col_at]
        vt[:HD] = tile[1].reshape(2 * TILE, HD).T
        scores = [
            [
                lax.dot_general(tile[0, u], q[k, s], (((1,), (1,)), ((), ())), preferred_element_type=jnp.float32)
                for u in range(2)
            ]
            for s in range(2)
        ]
        for s in range(2):
            old = top[k, s, :1]
            new = old
            for u in range(2):
                best = jnp.max(scores[s][u], axis=0, keepdims=True)
                new = jnp.maximum(new, best - (off if u == s else off_time))
            p = [
                jnp.exp2((scores[s][u] - (new + (off if u == s else off_time))) * scale).astype(jnp.bfloat16)
                for u in range(2)
            ]
            fix = jnp.exp2((old - new) * scale)
            add = jnp.dot(vt[...], jnp.concatenate(p, axis=0), preferred_element_type=jnp.float32)
            acc[k, s] = acc[k, s] * fix + add
            top[k, s] = jnp.broadcast_to(new, (8, TILE))

    def conclude(k):
        for s in range(2):
            o[k, s] = (acc[k, s, :HD] / acc[k, s, HD : HD + 1]).T.astype(jnp.bfloat16)
        for i in range(8):
            src, dst, copy = give_back(k, i)
            if i == 0:
                pl.when(y_hi == c)(pltpu.make_async_copy(src, dst, o_recv.at[k]).start)
                pl.when(y_hi != c)(copy.start)
            else:
                copy.start()

    steps = plan(far, wide)
    last = {}
    for n, (events, pick) in enumerate(steps):
        if pick:
            last[pick[0]] = n

    def one_step(n, carry):
        code = jnp.int32(-1)
        for m, (events, pick) in enumerate(steps):

            @pl.when(n == m)
            def _():
                for event in events:
                    communicate(event)
                if pick:
                    arrive(*pick)

            if pick:
                code = jnp.where(n == m, pick[0] * 9 + PLACES.index(pick[1]), code)

        @pl.when((code >= 0) & ((code % 9 < 6) | receiver) & ((code % 9 != 8) | halo_from))
        def _():
            attention(code // 9, code % 9)

        for k in range(SLOTS):
            pl.when(n == last[k])(lambda: conclude(k))
        return carry

    lax.fori_loop(0, len(steps), one_step, 0)

    for k in range(SLOTS):
        wait_for(back.at[pl.ds(k * CHIPS, CHIPS)], o_recv.at[k])
    for e in range(HEADS):
        out[:, e * HD : (e + 1) * HD] = back[rank[e]]

    scatter_queries(sent)
    for k in range(SLOTS):
        scatter(k, sent)
        for part_ in range(2):
            first_hop(k, part_).wait_send()
        own_share(k).wait_send()
        for i in range(8):
            copy = give_back(k, i)[2]
            if i == 0:
                pl.when(y_hi != c)(copy.wait_send)
            else:
                copy.wait_send()
    for k in range(far):
        for hop in range(2, 6 if k < wide else 5):
            for part_ in range(2):
                next_hop(k, hop, part_).wait_send()
        mid_share(k).wait_send()
        for part_ in range(2):
            for n in range(2 if k < min(wide, far - 1) else 1):
                pl.when(sender)(aside(k, n, part_).wait_send)
            pl.when(receiver)(side_share(k, part_).wait_send)
            if k == far - 1 and k < wide:
                pl.when(halo_to)(halo(k, part_).wait_send)


def run(far, wide, rank, barred, qh, kvh):
    dma = pltpu.SemaphoreType.DMA
    bf16, f32 = jnp.bfloat16, jnp.float32
    return pl.pallas_call(
        functools.partial(kernel, far, wide),
        out_shape=jax.ShapeDtypeStruct((PART, HEADS * HD), bf16),
        in_specs=[SMEM, SMEM, ANY, ANY],
        out_specs=VMEM,
        scratch_shapes=[
            pltpu.VMEM((SLOTS, 2, TILE, HD), bf16),
            pltpu.VMEM((SLOTS, 3, 3, 2, 2, TILE, HD), bf16),
            pltpu.VMEM((SLOTS, 2, 2, 2, TILE, HD), bf16),
            pltpu.VMEM((HD + 16, 2 * TILE), bf16),
            pltpu.VMEM((SLOTS, 2, 8, TILE), f32),
            pltpu.VMEM((SLOTS, 2, HD + 16, TILE), f32),
            pltpu.VMEM((SLOTS, 2, TILE, HD), bf16),
            pltpu.VMEM((HEADS, PART, HD), bf16),
            dma((SLOTS, 2, CHIPS)),
            dma((CHIPS,)),
            dma((SLOTS, 2)),
            dma,
            dma((SLOTS, 5, 2)),
            dma((SLOTS, 5, 2)),
            dma((SLOTS,)),
            dma((SLOTS,)),
            dma((SLOTS,)),
            dma((SLOTS,)),
            dma((SLOTS, 2, 2)),
            dma((SLOTS, 2, 2)),
            dma((SLOTS, 2)),
            dma((SLOTS, 2)),
            dma((2,)),
            dma((2,)),
            dma((SLOTS, 8)),
            dma((SLOTS,)),
        ],
        compiler_params=pltpu.CompilerParams(collective_id=far * 4 + wide, has_side_effects=True, vmem_limit_bytes=48 << 20),
        name=f"tile_attention{far}{wide}",
    )(rank, barred, qh, kvh)


def shards(queries, keys, values, windows):
    form, rank, barred, qh, kvh = pack(windows, queries, keys, values)
    forms = [(0, 0), (1, 0), (1, 1), (2, 1), (2, 2), (3, 2), (3, 3)]
    return lax.switch(form, [functools.partial(run, *f) for f in forms], rank, barred, qh, kvh)


def solution(mesh):
    tokens = P(("slab", "head"), None)
    return jax.shard_map(
        shards, mesh=mesh, in_specs=(tokens, tokens, tokens, P()), out_specs=tokens, check_vma=False
    )
```

```python
import functools

import jax
import jax.numpy as jnp
from jax import lax
from jax.experimental import pallas as pl
from jax.experimental.pallas import tpu as pltpu
from jax.sharding import PartitionSpec as P

MESH = pl.DeviceIdType.MESH
ANY = pl.BlockSpec(memory_space=pl.ANY)
SMEM = pl.BlockSpec(memory_space=pltpu.SMEM)
VMEM = pl.BlockSpec(memory_space=pltpu.VMEM)
HEADS, HD, TILE, PART = 24, 128, 384, 96
SLOTS, CHIPS = 3, 8
LOG2E = 1.4426950408889634


def coords():
    slab, head = lax.axis_index("slab"), lax.axis_index("head")
    x, z, y_hi = slab // 16, (slab // 2) % 8, slab % 2
    return x, y_hi * 2 + head // 2, z, head % 2


def device(x, y, z, c):
    return ((x * 8 + z) * 2 + y // 2, (y % 2) * 2 + c)


def remote(src, dst, send, recv, to):
    return pltpu.make_async_remote_copy(
        src_ref=src, dst_ref=dst, send_sem=send, recv_sem=recv, device_id=to, device_id_type=MESH
    )


def greet(devices):
    barrier = pltpu.get_barrier_semaphore()
    for to in devices:
        pl.semaphore_signal(barrier, 1, device_id=to, device_id_type=MESH)
    pl.semaphore_wait(barrier, len(devices))


def group(x, y, z, c):
    return [
        device((x + 2 * i) % 4, (y + m) % 4, z, (c + n) % 2)
        for i in range(2)
        for m in range(4)
        for n in range(2)
        if (i, m, n) != (0, 0, 0)
    ]


def pack_kernel(reach, q_hbm, k_hbm, v_hbm, qh, kvh, rank, barred, form, windows, count, q_in, k_in, v_in, sem):
    look = pltpu.make_async_copy(reach, windows, sem.at[3])
    look.start()
    loads = [
        pltpu.make_async_copy(src, dst, sem.at[i])
        for i, (src, dst) in enumerate([(k_hbm, k_in), (v_hbm, v_in), (q_hbm, q_in)])
    ]
    for load in loads:
        load.start()
    for b in range(8):
        count[b] = 0
    look.wait()
    key = [windows[1, e] * 4 + windows[2, e] * 2 + windows[0, e] for e in range(HEADS)]
    for e in range(HEADS):
        count[key[e]] = count[key[e]] + 1
    ahead = jnp.int32(0)
    for b in reversed(range(8)):
        here = count[b]
        count[b] = ahead
        ahead += here
    place = []
    for e in range(HEADS):
        r = count[key[e]]
        count[key[e]] = r + 1
        place.append(r)
    tall = both = jnp.int32(0)
    for e in range(HEADS):
        r = place[e]
        rank[e] = r
        tall += windows[1, e]
        both += windows[1, e] * windows[2, e]
        for axis in range(3):
            barred[r, axis] = jnp.where(windows[axis, e] > 0, 0.0, 1e30).astype(jnp.float32)
    far = (tall + CHIPS - 1) // CHIPS
    form[0] = jnp.where(far == 0, 0, 2 * far - 1 + (both > CHIPS * (far - 1)).astype(jnp.int32))
    for load in loads:
        load.wait()
    for e in range(HEADS):
        r = place[e]
        cols = pl.ds(e * HD, HD)
        qh[r] = q_in[:, cols]
        kvh[r, 0] = k_in[:, cols]
        kvh[r, 1] = v_in[:, cols]


def pack(windows, queries, keys, values):
    qh, kvh, rank, barred, form = pl.pallas_call(
        pack_kernel,
        out_shape=(
            jax.ShapeDtypeStruct((HEADS, PART, HD), jnp.bfloat16),
            jax.ShapeDtypeStruct((HEADS, 2, PART, HD), jnp.bfloat16),
            jax.ShapeDtypeStruct((HEADS,), jnp.int32),
            jax.ShapeDtypeStruct((HEADS, 3), jnp.float32),
            jax.ShapeDtypeStruct((1,), jnp.int32),
        ),
        in_specs=[ANY, ANY, ANY, ANY],
        out_specs=(VMEM, VMEM, SMEM, SMEM, SMEM),
        scratch_shapes=[pltpu.SMEM((3, HEADS), jnp.int32), pltpu.SMEM((8,), jnp.int32)]
        + [pltpu.VMEM((PART, HEADS * HD), jnp.bfloat16)] * 3
        + [pltpu.SemaphoreType.DMA((4,))],
        name="pack",
    )(windows.T, queries, keys, values)
    return form[0], rank, barred, qh.reshape(SLOTS, CHIPS, PART, HD), kvh.reshape(SLOTS, CHIPS, 2, PART, HD)


def plan(far, wide):
    def hops(k, hop):
        return [("forward" if hop < 5 else "near", k, hop, part) for part in range(2)]

    if far == 0:
        main = [("begin", 0), ("ask", 0), ("begin", 1), ("queries", 0), ("begin", 2)]
    else:
        main = [("begin", 0)] + hops(0, 2) + [("ask", 0)] + hops(0, 3) + [("begin", 1)] + hops(0, 4) + [("queries", 0)]
        if far == 1:
            main.append(("begin", 2))
        for k in range(1, far):
            main += hops(k, 2) + hops(k - 1, 5) + hops(k, 3)
            if (far, k) == (3, 1):
                main.append(("begin", 2))
            if k - 1 < wide:
                main.append(("finish", k - 1))
            main += hops(k, 4)
            if far == 2:
                main.append(("begin", 2))
            main += [("share", k - 1, 0), ("share", k - 1, 1)]
        main += hops(far - 1, 5) + [("finish", far - 1) if far <= wide else None, None, None]
        main += [("share", far - 1, 0), ("share", far - 1, 1)]

    def ready(event):
        what, k = event[0], event[1]
        if what == "queries":
            return [(0, 0, "own"), (0, 0, "inner"), (0, 0, "outer"), (0, 1, "own"), (0, 1, "inner")] + (
                [] if far > 1 else [(3, 1, "outer")]
            )
        if what == "begin" and k == 2:
            return [(0, 2, "own"), (1, 2, "inner")] + ([] if far > 2 else [(3, 2, "outer")])
        if what == "forward" and event[2:] == (2, 1) and k > 0:
            return [(0, k, "outer")]
        if what == "near" and event[3] == 1:
            return [(0, k, "near inner"), (1, k, "near own")]
        if what == "finish":
            return [(0, k, "near outer")]
        if what == "share" and event[2] == 1:
            return [(0, k, "side inner"), (1, k, "side own")] + ([(3, k, "side outer")] if k < wide else [])
        return []

    steps, pool = [], []
    n = 0
    while n < len(main) or pool:
        events = []
        if n < len(main) and main[n]:
            events.append(main[n])
            pool += [(n + late, len(pool), k, what) for late, k, what in ready(main[n])]
        pool.sort(key=lambda p: p[0])
        pick = None
        if pool and (pool[0][0] <= n or n >= len(main)):
            pick = pool.pop(0)[2:]
        steps.append((events, pick))
        n += 1
    return steps


PLACES = ["own", "inner", "outer", "near own", "near inner", "near outer", "side own", "side inner", "side outer"]


def kernel(
    far, wide, rank, barred, qh, kvh, out,
    q, kv, relay, vt, top, acc, o, back,
    a_send, q_send, kv_recv, q_recv, hop_send, hop_recv, own_send, own_recv,
    mid_send, mid_recv, x_send, x_recv, xs_send, xs_recv, halo_send, halo_recv, o_send, o_recv,
):
    x, y, z, c = coords()
    z_hi, x_lo, t = z // 4, x % 2, x // 2
    up, down = (z + 1) % 8, (z + 7) % 8
    twin = device(x, y, z, 1 - c)
    side = device(x + 1 - 2 * x_lo, y, z, c)
    ahead = device(x, y, jnp.where(c == 0, up, down), c)
    first = device(x, y, jnp.where(c == 0, down, up), 1 - c)
    barrier = pltpu.get_barrier_semaphore()
    partners = group(x, y, z, c) + [
        device(x, y, up, c), device(x, y, up, 1 - c), device(x, y, down, c), device(x, y, down, 1 - c), side
    ]
    for to in partners:
        pl.semaphore_signal(barrier, 1, device_id=to, device_id_type=MESH)

    pl.semaphore_wait(barrier, len(partners))

    y_hi = y // 2
    part = (y % 2) * 2 + c
    me = t * 4 + y
    rows = pl.ds(part * PART, PART)
    def spread(act):
        def one(i, src, dst, sem, recv, chip):
            copy = remote(src, dst, sem, recv, device((chip // 4) * 2 + x_lo, chip % 4, z, y_hi))
            if i > 0:
                act(copy)
            else:
                pl.when(c != y_hi)(lambda: act(copy))
                if act is start:
                    pl.when(c == y_hi)(pltpu.make_async_copy(src, dst, recv).start)

        return one

    def start(copy):
        copy.start()

    def sent(copy):
        copy.wait_send()

    def scatter(k, act):
        for p in range(2):
            for i in range(CHIPS):
                chip = (me + i) % CHIPS
                spread(act)(i, kvh.at[k, chip, p], kv.at[k, 1, 1, p, t, rows], a_send.at[k, p, i], kv_recv.at[k, p], chip)

    def scatter_queries(act):
        for i in range(CHIPS):
            chip = (me + i) % CHIPS
            spread(act)(i, qh.at[:, chip], q.at[:, t, rows], q_send.at[i], q_recv, chip)

    scatter(0, start)
    top[...] = jnp.full_like(top, -1e30)
    acc[...] = jnp.zeros_like(acc)
    vt[HD:] = jnp.ones((16, 2 * TILE), jnp.bfloat16)

    outer = c * 2
    inner = 2 - outer
    near = 2 - 2 * z_hi
    z_next = jnp.where(c == 0, up, down)
    near_next = 2 - 2 * (z_next // 4)
    sender = x_lo == z_hi
    receiver = jnp.logical_not(sender)
    w_edge = jnp.where(c == 0, z % 4 > 0, z % 4 < 3)
    halo_to = receiver & jnp.where(c == 0, z % 4 < 3, z % 4 > 0)
    halo_from = receiver & w_edge

    def wait_for(place, sem):
        pltpu.make_async_copy(place, place, sem).wait()

    def landing(k, hop, part, near_of):
        if hop == 1:
            return kv.at[k, 1, outer, part]
        if hop < 4:
            return relay.at[k, hop - 2, part]
        return kv.at[k, near_of, inner if hop == 4 else outer, part]

    def hop_wait(k, hop, part):
        wait_for(landing(k, hop, part, near), hop_recv.at[k, hop - 1, part])

    def first_hop(k, part):
        return remote(
            kv.at[k, 1, 1, part], kv.at[k, 1, inner, part], hop_send.at[k, 0, part], hop_recv.at[k, 0, part], first
        )

    def next_hop(k, hop, part):
        return remote(
            landing(k, hop - 1, part, near),
            landing(k, hop, part, near_next),
            hop_send.at[k, hop - 1, part],
            hop_recv.at[k, hop - 1, part],
            ahead,
        )

    def own_share(k):
        return remote(kv.at[k, 1, 1], kv.at[k, 1, outer], own_send.at[k], own_recv.at[k], twin)

    def mid_share(k):
        return remote(kv.at[k, near, inner], kv.at[k, near, 1], mid_send.at[k], mid_recv.at[k], twin)

    def aside(k, n, part):
        place = inner if n == 0 else outer
        return remote(
            kv.at[k, near, place, part], kv.at[k, 2 - near, place, part], x_send.at[k, n, part], x_recv.at[k, n, part], side
        )

    def side_wait(k, n, part):
        wait_for(kv.at[k, 2 - near, inner if n == 0 else outer, part], x_recv.at[k, n, part])

    def side_share(k, part):
        place = kv.at[k, 2 - near, inner, part]
        return remote(place, kv.at[k, 2 - near, 1, part], xs_send.at[k, part], xs_recv.at[k, part], twin)

    def halo(k, part):
        place = kv.at[k, 2 - near, inner, part]
        return remote(place, kv.at[k, 2 - near, outer, part], halo_send.at[part], halo_recv.at[part], ahead)

    def give_back(k, i):
        n = (t * 4 + part + i) % 8
        to = device((n // 4) * 2 + x_lo, c * 2 + (n % 4) // 2, z, n % 2)
        src = o.at[k, n // 4, pl.ds((n % 4) * PART, PART)]
        dst = back.at[k * CHIPS + me]
        return src, dst, remote(src, dst, o_send.at[k, i], o_recv.at[k], to)

    def communicate(event):
        what, k = event[0], event[1]
        if what == "begin":
            for part in range(2):
                wait_for(kv.at[k, 1, 1, part], kv_recv.at[k, part])
                first_hop(k, part).start()
            own_share(k).start()
            if k < 2:
                scatter(k + 1, start)
        elif what == "ask":
            scatter_queries(start)
        elif what == "queries":
            wait_for(q, q_recv)
        elif what == "forward":
            hop, part = event[2:]
            hop_wait(k, hop - 1, part)
            next_hop(k, hop, part).start()
        elif what == "near":
            part = event[3]
            hop_wait(k, 4, part)
            if k < wide:
                next_hop(k, 5, part).start()
            pl.when(sender)(aside(k, 0, part).start)
            if part == 1:
                mid_share(k).start()
        elif what == "finish":
            for part in range(2):
                hop_wait(k, 5, part)
                if k < far - 1:
                    pl.when(sender)(aside(k, 1, part).start)
        else:
            part = event[2]

            @pl.when(receiver)
            def _():
                side_wait(k, 0, part)
                side_share(k, part).start()

            if k == far - 1 and k < wide:
                pl.when(halo_to)(halo(k, part).start)

    def arrive(k, what):
        if what == "inner":
            wait_for(kv.at[k, 1, inner], own_recv.at[k])
        elif what == "outer" and k >= far:
            for part in range(2):
                hop_wait(k, 1, part)
        elif what == "near own":
            wait_for(kv.at[k, near, 1], mid_recv.at[k])
        elif what == "side own":

            @pl.when(receiver)
            def _():
                for part in range(2):
                    wait_for(kv.at[k, 2 - near, 1, part], xs_recv.at[k, part])

        elif what == "side outer":

            @pl.when(halo_from if k == far - 1 else receiver)
            def _():
                for part in range(2):
                    if k == far - 1:
                        wait_for(kv.at[k, 2 - near, outer, part], halo_recv.at[part])
                    else:
                        side_wait(k, 1, part)

    scale = HD ** (-0.5) * LOG2E

    def attention(k, place):
        dh, dw = place // 3, place % 3
        row = k * CHIPS + me
        row_at = jnp.where(dh == 0, 1, jnp.where(dh == 1, near, 2 - near))
        col_at = jnp.where(dw == 0, 1, jnp.where(dw == 1, inner, outer))
        off = barred[row, 1] * jnp.minimum(dh, 1).astype(jnp.float32)
        off += barred[row, 2] * jnp.minimum(dw, 1).astype(jnp.float32)
        off += jnp.where((dw == 2) & jnp.logical_not(w_edge), 1e30, 0.0)
        off_time = off + barred[row, 0]
        tile = kv.at[k, row_at, col_at]
        vt[:HD] = tile[1].reshape(2 * TILE, HD).T
        scores = [
            [
                lax.dot_general(tile[0, u], q[k, s], (((1,), (1,)), ((), ())), preferred_element_type=jnp.float32)
                for u in range(2)
            ]
            for s in range(2)
        ]
        for s in range(2):
            old = top[k, s, :1]
            new = old
            for u in range(2):
                best = jnp.max(scores[s][u], axis=0, keepdims=True)
                new = jnp.maximum(new, best - (off if u == s else off_time))
            p = [
                jnp.exp2((scores[s][u] - (new + (off if u == s else off_time))) * scale).astype(jnp.bfloat16)
                for u in range(2)
            ]
            fix = jnp.exp2((old - new) * scale)
            add = jnp.dot(vt[...], jnp.concatenate(p, axis=0), preferred_element_type=jnp.float32)
            acc[k, s] = acc[k, s] * fix + add
            top[k, s] = jnp.broadcast_to(new, (8, TILE))

    def conclude(k):
        for s in range(2):
            o[k, s] = (acc[k, s, :HD] / acc[k, s, HD : HD + 1]).T.astype(jnp.bfloat16)
        for i in range(8):
            src, dst, copy = give_back(k, i)
            if i == 0:
                pl.when(y_hi == c)(pltpu.make_async_copy(src, dst, o_recv.at[k]).start)
                pl.when(y_hi != c)(copy.start)
            else:
                copy.start()

    steps = plan(far, wide)
    last = {}
    for n, (events, pick) in enumerate(steps):
        if pick:
            last[pick[0]] = n

    def one_step(n, carry):
        code = jnp.int32(-1)
        for m, (events, pick) in enumerate(steps):

            @pl.when(n == m)
            def _():
                for event in events:
                    communicate(event)
                if pick:
                    arrive(*pick)

            if pick:
                code = jnp.where(n == m, pick[0] * 9 + PLACES.index(pick[1]), code)

        @pl.when((code >= 0) & ((code % 9 < 6) | receiver) & ((code % 9 != 8) | halo_from))
        def _():
            attention(code // 9, code % 9)

        for k in range(SLOTS):
            pl.when(n == last[k])(lambda: conclude(k))
        return carry

    lax.fori_loop(0, len(steps), one_step, 0)

    for k in range(SLOTS):
        wait_for(back.at[pl.ds(k * CHIPS, CHIPS)], o_recv.at[k])
    for e in range(HEADS):
        out[:, e * HD : (e + 1) * HD] = back[rank[e]]

    scatter_queries(sent)
    for k in range(SLOTS):
        scatter(k, sent)
        for part_ in range(2):
            first_hop(k, part_).wait_send()
        own_share(k).wait_send()
        for i in range(8):
            copy = give_back(k, i)[2]
            if i == 0:
                pl.when(y_hi != c)(copy.wait_send)
            else:
                copy.wait_send()
    for k in range(far):
        for hop in range(2, 6 if k < wide else 5):
            for part_ in range(2):
                next_hop(k, hop, part_).wait_send()
        mid_share(k).wait_send()
        for part_ in range(2):
            for n in range(2 if k < min(wide, far - 1) else 1):
                pl.when(sender)(aside(k, n, part_).wait_send)
            pl.when(receiver)(side_share(k, part_).wait_send)
            if k == far - 1 and k < wide:
                pl.when(halo_to)(halo(k, part_).wait_send)


def run(far, wide, rank, barred, qh, kvh):
    dma = pltpu.SemaphoreType.DMA
    bf16, f32 = jnp.bfloat16, jnp.float32
    return pl.pallas_call(
        functools.partial(kernel, far, wide),
        out_shape=jax.ShapeDtypeStruct((PART, HEADS * HD), bf16),
        in_specs=[SMEM, SMEM, ANY, ANY],
        out_specs=VMEM,
        scratch_shapes=[
            pltpu.VMEM((SLOTS, 2, TILE, HD), bf16),
            pltpu.VMEM((SLOTS, 3, 3, 2, 2, TILE, HD), bf16),
            pltpu.VMEM((SLOTS, 2, 2, 2, TILE, HD), bf16),
            pltpu.VMEM((HD + 16, 2 * TILE), bf16),
            pltpu.VMEM((SLOTS, 2, 8, TILE), f32),
            pltpu.VMEM((SLOTS, 2, HD + 16, TILE), f32),
            pltpu.VMEM((SLOTS, 2, TILE, HD), bf16),
            pltpu.VMEM((HEADS, PART, HD), bf16),
            dma((SLOTS, 2, CHIPS)),
            dma((CHIPS,)),
            dma((SLOTS, 2)),
            dma,
            dma((SLOTS, 5, 2)),
            dma((SLOTS, 5, 2)),
            dma((SLOTS,)),
            dma((SLOTS,)),
            dma((SLOTS,)),
            dma((SLOTS,)),
            dma((SLOTS, 2, 2)),
            dma((SLOTS, 2, 2)),
            dma((SLOTS, 2)),
            dma((SLOTS, 2)),
            dma((2,)),
            dma((2,)),
            dma((SLOTS, 8)),
            dma((SLOTS,)),
        ],
        compiler_params=pltpu.CompilerParams(collective_id=far * 4 + wide, has_side_effects=True, vmem_limit_bytes=48 << 20),
        name=f"tile_attention{far}{wide}",
    )(rank, barred, qh, kvh)


def shards(queries, keys, values, windows):
    form, rank, barred, qh, kvh = pack(windows, queries, keys, values)
    forms = [(0, 0), (1, 0), (1, 1), (2, 1), (2, 2), (3, 2), (3, 3)]
    return lax.switch(form, [functools.partial(run, *f) for f in forms], rank, barred, qh, kvh)


def solution(mesh):
    tokens = P(("slab", "head"), None)
    return jax.shard_map(
        shards, mesh=mesh, in_specs=(tokens, tokens, tokens, P()), out_specs=tokens, check_vma=False
    )
```
